32 devices in a mesh: lat: 8 (over z, x), lon: 4 (over y, core).
Axes of the slice: x: 2, y: 2, z: 4, core: 2. Of those that a mesh axis runs over, the one named last changes fastest.
Arguments:
- thickness: float32 [2, 1024, 8192], P(None, 'lat', 'lon'), may hold values from 0.5 to 1.5
- winds: float32 [2, 2, 1024, 8192], P(None, None, 'lat', 'lon'), may hold values from -3 to 3
- terrain: float32 [1024, 8192], P('lat', 'lon'), may hold values from -1.5 to 1.5
- cutoffs: int32 [342], replicated, may hold values from 1 to 4096, as said below
Outputs:
- new_thickness: float32 [2, 1024, 8192], P(None, 'lat', 'lon')
- new_winds: float32 [2, 2, 1024, 8192], P(None, None, 'lat', 'lon')
The draws below stay inside these ranges and needn't reach their ends.
Inputs may be any that keep to these rules, and one draw needn't show every extreme that they name: cutoffs[p] is the count of the lowest zonal wavenumbers kept on cap row p (the 171 southernmost rows from south to north, then the 171 northernmost).
All inputs are finite; a program needn't handle non-finite values.
Results may differ from the reference program's by a relative error of at most 0.0003.
Values sent between devices are 32-bit elements; how exact they have to be, the bound alone decides.
A program may use at most 128 MiB of HBM per device.

```python
import math
import jax
import jax.numpy as jnp
from jax import lax

ROWS_DEV = 128
NLON = 8192
LEVELS = 2
STEPS = 1
NLAT = 1024
POLAR_ROWS = 171
N_LAT = 8


def draw_cutoffs(key, part):
    offsets = jnp.arange(POLAR_ROWS, dtype=jnp.int32)
    distance = jnp.concatenate([offsets, POLAR_ROWS - 1 - offsets])
    nyquist = NLON // 2
    ceiling = 1 + (nyquist - 1) * distance // max(POLAR_ROWS - 1, 1)
    jitter = jax.random.randint(key, (2 * POLAR_ROWS,), 0, 1048576, dtype=jnp.int32)
    lowered = ceiling - jitter % (ceiling // 2 + 1)
    return jnp.where(distance == POLAR_ROWS - 1, ceiling, lowered).astype(jnp.int32)


def levels(key, dims, shards, least, top_value):
    def one(position, parts):
        steps = jax.random.uniform(jax.random.fold_in(jax.random.fold_in(key, 6), position), (parts,), jnp.float32, least / len(shards), top_value / len(shards))
        return jnp.repeat(jnp.exp(steps), dims[position] // parts).reshape((-1,) + (1,) * (len(dims) - position - 1))

    level = one(*shards[0])
    for cut in shards[1:]:
        level = level * one(*cut)
    return level


def bell_draw(stream_key, shape, width, limit, split=(), kind=jnp.bfloat16):
    entries = width * jax.random.normal(stream_key, shape, jnp.float32)
    if split:
        entries = entries * levels(stream_key, shape, split, -0.22, 0.18)
    return jnp.clip(entries, -limit, limit).astype(kind)


def setup_inputs(seed: int = 0) -> dict:
    key_list = jax.random.split(jax.random.key(seed), 5)
    return {
        "thickness": jnp.clip(0.5 + 1.0 * jax.random.uniform(key_list[0], (LEVELS, NLAT, NLON), jnp.float32) ** levels(key_list[0], (LEVELS, NLAT, NLON), ((1, 8), (2, 4)), -0.2, 0.2), 0.5, 1.5),
        "winds": bell_draw(key_list[1], (2, LEVELS, NLAT, NLON), 0.5, 3.0, ((2, 8), (3, 4)), jnp.float32),
        "terrain": bell_draw(key_list[2], (NLAT, NLON), 0.3, 1.5, ((0, 8), (1, 4)), jnp.float32),
        "cutoffs": draw_cutoffs(jax.random.fold_in(key_list[4], 71), 0),
    }


GRAVITY = 1.0
DENSITY_RATIO = 0.9
CORIOLIS = 1.0


def stencil_tendency(padded, row_start, total_rows, circle):
    row_count = padded.shape[1] - 2
    thickness = padded[0:2]
    zonal_wind = padded[2:4]
    ground = padded[6]
    row_ids = row_start - 1 + jnp.arange(row_count + 2, dtype=jnp.int32)
    spacing = math.pi / total_rows
    centre_lat = -0.5 * math.pi + (row_ids.astype(jnp.float32) + 0.5) * spacing
    face_lat = -0.5 * math.pi + (row_ids.astype(jnp.float32) + 1.0) * spacing
    face_live = jnp.where((row_ids >= 0) & (row_ids < total_rows - 1), 1.0, 0.0).astype(jnp.float32)
    centre_cos = jnp.cos(centre_lat)
    face_cos = jnp.cos(face_lat) * face_live
    face_inverse = face_live / (face_cos + (1.0 - face_live))
    merid_step = circle / (2.0 * total_rows)
    merid_wind = padded[4:6] * face_live[None, :, None]
    inner_cosine = centre_cos[1:-1][None, :, None]

    flux_east = 0.5 * (thickness[:, :, :-1] + thickness[:, :, 1:]) * zonal_wind[:, :, :-1]
    flux_north = 0.5 * (thickness[:, :-1, :] + thickness[:, 1:, :]) * merid_wind[:, :-1, :] * face_cos[:-1][None, :, None]
    converge = (flux_east[:, 1:-1, 1:] - flux_east[:, 1:-1, :-1]) + (flux_north[:, 1:, 1:-1] - flux_north[:, :-1, 1:-1]) / merid_step
    thick_tend = -converge / inner_cosine

    kinetic = 0.25 * (zonal_wind[:, 1:, 1:] ** 2 + zonal_wind[:, 1:, :-1] ** 2 + merid_wind[:, 1:, 1:] ** 2 + merid_wind[:, :-1, 1:] ** 2)
    upper_layer = thickness[0, 1:, 1:]
    lower_layer = thickness[1, 1:, 1:]
    surface = ground[1:, 1:]
    potential = jnp.stack([GRAVITY * (upper_layer + lower_layer + surface), GRAVITY * (DENSITY_RATIO * upper_layer + lower_layer + surface)])
    energy = kinetic + potential

    merid_diff = merid_wind[:, :-1, 1:] - merid_wind[:, :-1, :-1]
    zonal_diff = zonal_wind[:, 1:, :-1] * centre_cos[1:][None, :, None] - zonal_wind[:, :-1, :-1] * centre_cos[:-1][None, :, None]
    absolute = CORIOLIS * jnp.sin(face_lat[:-1])[None, :, None] + (merid_diff - zonal_diff / merid_step) * face_inverse[:-1][None, :, None]

    merid_mean = 0.25 * (merid_wind[:, 1:-1, 1:-1] + merid_wind[:, 1:-1, 2:] + merid_wind[:, :-2, 1:-1] + merid_wind[:, :-2, 2:])
    zonal_mean = 0.25 * (zonal_wind[:, 1:-1, 1:-1] + zonal_wind[:, 1:-1, :-2] + zonal_wind[:, 2:, 1:-1] + zonal_wind[:, 2:, :-2])
    centre_energy = energy[:, :-1, :-1]
    east_energy = energy[:, :-1, 1:]
    north_energy = energy[:, 1:, :-1]
    zonal_tend = 0.5 * (absolute[:, 1:, 1:] + absolute[:, :-1, 1:]) * merid_mean - (east_energy - centre_energy) / inner_cosine
    merid_tend = (-0.5 * (absolute[:, 1:, 1:] + absolute[:, 1:, :-1]) * zonal_mean - (north_energy - centre_energy) / merid_step) * face_live[1:-1][None, :, None]
    return jnp.concatenate([thick_tend, zonal_tend, merid_tend], axis=0)


def full_tendency(state, terrain):
    padded_state = jnp.pad(state, ((0, 0), (1, 1), (0, 0)))
    padded_ground = jnp.pad(terrain, ((1, 1), (0, 0)))

    def one_band(index):
        anchor = (index * ROWS_DEV).astype(jnp.int32)
        block = lax.dynamic_slice_in_dim(padded_state, anchor, ROWS_DEV + 2, axis=1)
        ground = lax.dynamic_slice_in_dim(padded_ground, anchor, ROWS_DEV + 2, axis=0)
        stacked = jnp.concatenate([block, ground[None]], axis=0)
        wrapped = jnp.concatenate([stacked[:, :, -1:], stacked, stacked[:, :, :1]], axis=2)
        return stencil_tendency(wrapped, anchor, NLAT, NLON)

    pieces = lax.map(one_band, jnp.arange(N_LAT, dtype=jnp.int32))
    return jnp.transpose(pieces, (1, 0, 2, 3)).reshape(6, NLAT, NLON)


def polar_filter(tendency, cutoffs):
    caps = jnp.concatenate([tendency[:, :POLAR_ROWS], tendency[:, NLAT - POLAR_ROWS:]], axis=1)
    spectrum = jnp.fft.rfft(caps, axis=-1)
    wavenumber = jnp.arange(NLON // 2 + 1, dtype=jnp.int32)
    keep = wavenumber[None, :] < cutoffs[:, None]
    caps = jnp.fft.irfft(jnp.where(keep[None], spectrum, 0.0), n=NLON, axis=-1).astype(jnp.float32)
    middle = tendency[:, POLAR_ROWS:NLAT - POLAR_ROWS]
    return jnp.concatenate([caps[:, :POLAR_ROWS], middle, caps[:, POLAR_ROWS:]], axis=1)


def reference(thickness, winds, terrain, cutoffs):
    live = jnp.where(jnp.arange(NLAT, dtype=jnp.int32) < NLAT - 1, 1.0, 0.0).astype(jnp.float32)
    current = jnp.concatenate([thickness, winds[0], winds[1] * live[None, :, None]], axis=0)
    step_size = 0.1 * min(1.0, NLON / (2.0 * NLAT))
    for step_index in range(STEPS):
        anchor = current
        for fraction in (1.0 / 3.0, 0.5, 1.0):
            tendency = polar_filter(full_tendency(current, terrain), cutoffs)
            current = anchor + (fraction * step_size) * tendency
    return current[0:2], current[2:6].reshape(2, 2, NLAT, NLON)
```

```python
import functools
import math

import jax
import jax.numpy as jnp
import numpy as np
from jax import lax
from jax.experimental import pallas as pl
from jax.experimental.pallas import tpu as pltpu
from jax.sharding import PartitionSpec as P

GRAVITY = 1.0
DENSITY_RATIO = 0.9
CORIOLIS = 1.0
LANES = 128
TILE = 8
MESH = pl.DeviceIdType.MESH
LIMIT = 56 * 1024 * 1024


def stencil_kernel(state_ref, rows_ref, cols_ref, ground_ref, coef_ref, out_ref, pad, sems):
    row_count, col_count = state_ref.shape[1:]
    window = 512
    wide = window + 2 * LANES
    merid_inverse = out_merid_inverse(col_count, row_count)
    inner_rows, inner_cols = pl.ds(TILE, row_count), pl.ds(LANES, col_count)
    copies = [
        (state_ref, pad.at[0:6, inner_rows, inner_cols]),
        (ground_ref, pad.at[6, inner_rows, inner_cols]),
        (rows_ref.at[:, 0:TILE], pad.at[:, 0:TILE, inner_cols]),
        (rows_ref.at[:, TILE : 2 * TILE], pad.at[:, pl.ds(TILE + row_count, TILE), inner_cols]),
        (cols_ref.at[:, :, 0:LANES], pad.at[:, :, 0:LANES]),
        (cols_ref.at[:, :, LANES : 2 * LANES], pad.at[:, :, pl.ds(LANES + col_count, LANES)]),
    ]
    started = [pltpu.make_async_copy(a, b, sems.at[i]) for i, (a, b) in enumerate(copies)]
    for copy in started:
        copy.start()
    for copy in started:
        copy.wait()

    def east(x):
        return pltpu.roll(x, wide - 1, 1)

    def west(x):
        return pltpu.roll(x, 1, 1)

    def triple(x):
        return x[TILE - 1 : 2 * TILE - 1], x[TILE : 2 * TILE], x[TILE + 1 : 2 * TILE + 1]

    def one(step, _):
        tile = step // (col_count // window)
        part = step % (col_count // window)
        rows = pl.ds(pl.multiple_of(tile * TILE, TILE), 3 * TILE)
        cols = pl.ds(pl.multiple_of(part * window, window), wide)

        def field(k):
            return triple(pad[k, rows, cols])

        def coef(k):
            return tuple(jnp.tile(x, (1, wide // LANES)) for x in triple(coef_ref[k, rows, :]))

        cm, co, cp = coef(0)
        inv = coef(1)[1]
        em, eo, _ = coef(2)
        sm, so, _ = coef(3)
        fm, fo, _ = coef(4)
        live = coef(5)[1]
        h0 = field(0)
        h1 = field(1)
        ground = field(6)
        out_rows = pl.ds(pl.multiple_of(tile * TILE, TILE), TILE)
        out_cols = pl.ds(pl.multiple_of(part * window, window), window)
        for layer in range(2):
            hm, ho, hp = h0 if layer == 0 else h1
            um, uo, up = field(2 + layer)
            vm, vo, vp = field(4 + layer)
            ratio = 1.0 if layer == 0 else DENSITY_RATIO
            flux = 0.5 * (ho + east(ho)) * uo
            north = 0.5 * (ho + hp) * vo * eo
            south = 0.5 * (hm + ho) * vm * em
            thick = -((flux - west(flux)) + (north - south) * merid_inverse) * inv
            squares = uo * uo
            energy = 0.25 * (squares + west(squares) + vo * vo + vm * vm) + (
                ratio * h0[1] + h1[1] + ground[1]
            )
            squares = up * up
            energy_north = 0.25 * (squares + west(squares) + vp * vp + vo * vo) + (
                ratio * h0[2] + h1[2] + ground[2]
            )
            curl_o = so + ((east(vo) - vo) - (up * cp - uo * co) * merid_inverse) * fo
            curl_m = sm + ((east(vm) - vm) - (uo * co - um * cm) * merid_inverse) * fm
            merid_sum = vo + vm
            zonal_sum = uo + up
            zonal = 0.125 * (curl_o + curl_m) * (merid_sum + east(merid_sum)) - (
                east(energy) - energy
            ) * inv
            merid = (
                -0.125 * (curl_o + west(curl_o)) * (zonal_sum + west(zonal_sum))
                - (energy_north - energy) * merid_inverse
            ) * live
            inside = slice(LANES, LANES + window)
            out_ref[layer, out_rows, out_cols] = thick[:, inside]
            out_ref[2 + layer, out_rows, out_cols] = zonal[:, inside]
            out_ref[4 + layer, out_rows, out_cols] = merid[:, inside]
        return 0

    lax.fori_loop(0, (row_count // TILE) * (col_count // window), one, 0)


def out_merid_inverse(col_count, row_count):
    circle = col_count * lax.axis_size("lon")
    total = row_count * lax.axis_size("lat")
    return 2.0 * total / circle


def stencil(state, rows, cols, ground, coefs):
    row_count, col_count = state.shape[1:]
    return pl.pallas_call(
        stencil_kernel,
        out_shape=jax.ShapeDtypeStruct(state.shape, jnp.float32),
        in_specs=[pl.BlockSpec(memory_space=pl.ANY)] * 4 + [pl.BlockSpec(memory_space=pltpu.VMEM)],
        out_specs=pl.BlockSpec(memory_space=pltpu.VMEM),
        scratch_shapes=[
            pltpu.VMEM((7, row_count + 2 * TILE, col_count + 2 * LANES), jnp.float32),
            pltpu.SemaphoreType.DMA((6,)),
        ],
        compiler_params=pltpu.CompilerParams(vmem_limit_bytes=LIMIT),
        name="stencil",
    )(state, rows, cols, ground, coefs)


def times(z, w):
    re, im = z
    wr, wi = w.real, w.imag
    if abs(wr) < 1e-12:
        return (None if im is None else im * (-wi), re * wi)
    if abs(wi) < 1e-12:
        return (re * wr, None if im is None else im * wr)
    if im is None:
        return (re * wr, re * wi)
    return (re * wr - im * wi, re * wi + im * wr)


def plus(a, b):
    return b if a is None else a if b is None else a + b


def minus(a, b):
    if b is None:
        return a
    return -b if a is None else a - b


def forward_real(x):
    n = len(x)
    if n == 2:
        return [(x[0] + x[1], None), (x[0] - x[1], None)]
    even, odd = forward_real(x[0::2]), forward_real(x[1::2])
    out = [None] * (n // 2 + 1)
    for k in range(n // 4 + 1):
        er, ei = even[k]
        tr, ti = (odd[k][0], odd[k][1]) if k == 0 else times(odd[k], np.exp(-2j * np.pi * k / n))
        out[k] = (plus(er, tr), plus(ei, ti))
        if k < n // 4:
            low = minus(ei, ti)
            out[n // 2 - k] = (minus(er, tr), None if low is None else -low)
    return out


def inverse_real(z):
    n = 2 * (len(z) - 1)
    if n == 2:
        return [z[0][0] + z[1][0], z[0][0] - z[1][0]]
    even, odd = [], []
    for k in range(n // 4 + 1):
        if k == n // 4:
            re, im = z[k]
            even.append((re + re, None))
            odd.append((-(im + im), None))
            continue
        ar, ai = z[k]
        br, bi = z[n // 2 - k]
        if k == 0:
            even.append((ar + br, None))
            odd.append((ar - br, None))
            continue
        even.append((plus(ar, br), minus(ai, bi)))
        odd.append(times((minus(ar, br), plus(ai, bi)), np.exp(2j * np.pi * k / n)))
    out = [None] * n
    out[0::2] = inverse_real(even)
    out[1::2] = inverse_real(odd)
    return out


def tables(circle):
    first = circle // LANES
    half = first // 2 + 1
    b = np.arange(LANES)
    angle = 2.0 * np.pi / LANES * (np.outer(b, b) % LANES)
    c, s = np.cos(angle), np.sin(angle)
    ahead = np.block([[c, -s], [s, c]])
    back = np.block([[c, s], [-s, c]]) / circle
    turn = 2.0 * np.pi / circle * np.outer(np.arange(half), b)
    padded = -(-half // TILE) * TILE
    twist = np.zeros((2, padded, LANES))
    twist[0, :half], twist[1, :half] = np.cos(turn), np.sin(turn)
    return [x.astype(np.float32) for x in (ahead, back, twist)]


class Plan:
    def __init__(self, lat_count, lon_count, row_count, polar):
        self.chunk = TILE * lon_count
        self.workers = lat_count // 2
        bands = -(-polar // row_count)
        self.chunks = [
            -(-min(row_count, polar - b * row_count) // self.chunk) for b in range(bands)
        ]
        pairs = {}
        for b in range(bands):
            for f in range(6):
                if bands == 2 and self.workers >= 4:
                    pairs[b, f] = f % 3 if b == 0 else (3 if f < 5 else 1)
                else:
                    pairs[b, f] = (6 * b + f) % self.workers
        self.slots = [[] for _ in range(self.workers)]
        self.where = {}
        for c in range(max(self.chunks)):
            for b in range(bands):
                for f in range(6):
                    if c < self.chunks[b]:
                        w = pairs[b, f]
                        self.where[b, c, f] = (w, len(self.slots[w]))
                        self.slots[w].append((b, c, f))
        self.most = max(len(x) for x in self.slots)
        self.partners = [set() for _ in range(self.workers)]
        for (b, _, _), (w, _) in self.where.items():
            self.partners[b].add(w)
            self.partners[w].add(b)


def filter_kernel(
    plan, tend, keep, ahead, behind, twist, back, taken, made, spec, sent, got, returned, home
):
    lat_count, lon_count = lax.axis_size("lat"), lax.axis_size("lon")
    lat, lon = lax.axis_index("lat"), lax.axis_index("lon")
    row_count, col_count = tend.shape[1:]
    circle = col_count * lon_count
    first = circle // LANES
    half = first // 2 + 1
    north = lat >= lat_count // 2
    band = jnp.where(north, lat_count - 1 - lat, lat)

    def real_band(b):
        return jnp.where(north, lat_count - 1 - b, b)

    def chunk_row(b, c):
        base = jnp.where(north, row_count - plan.chunks[b] * plan.chunk, 0)
        return base + c * plan.chunk

    barrier = pltpu.get_barrier_semaphore()
    for b in range(plan.workers):
        count = 0
        others = sorted(plan.partners[b])
        if not others:
            continue

        @pl.when(band == b)
        def _():
            count = 0
            for other in others:
                for hop in range(lon_count):
                    if other == b and hop == 0:
                        continue
                    pl.semaphore_signal(
                        barrier,
                        inc=1,
                        device_id=(real_band(other), lax.rem(lon + hop, lon_count)),
                        device_id_type=MESH,
                    )
                    count += 1
            pl.semaphore_wait(barrier, count)

    mine = pl.ds(pl.multiple_of(lon * col_count, LANES), col_count)
    for b in range(len(plan.chunks)):

        @pl.when(band == b)
        def _():
            for c in range(plan.chunks[b]):
                for f in range(6):
                    worker, slot = plan.where[b, c, f]
                    for hop in list(range(1, lon_count)) + [0]:
                        peer = lax.rem(lon + hop, lon_count)
                        start = pl.multiple_of(chunk_row(b, c) + peer * TILE, TILE)
                        source = tend.at[f, pl.ds(start, TILE), :]
                        target = taken.at[slot, :, mine]
                        if hop == 0 and worker == b:
                            pltpu.make_async_copy(source, target, got.at[slot]).start()
                        else:
                            pltpu.make_async_remote_copy(
                                src_ref=source,
                                dst_ref=target,
                                send_sem=sent.at[c * 6 + f],
                                recv_sem=got.at[slot],
                                device_id=(real_band(worker), peer),
                                device_id_type=MESH,
                            ).start()

    slot_count = jnp.int32(0)
    for w in range(plan.workers):
        slot_count = jnp.where(band == w, len(plan.slots[w]), slot_count)

    def one(slot, _):
        pltpu.make_async_copy(taken.at[slot], taken.at[slot], got.at[slot]).wait()
        parts = forward_real(
            [taken[slot, :, a * LANES : (a + 1) * LANES] for a in range(first)]
        )
        for k in range(half):
            re, im = parts[k]
            c, s = twist[0, k : k + 1, :], twist[1, k : k + 1, :]
            if im is None:
                tr, ti = re * c, -(re * s)
            else:
                tr, ti = re * c + im * s, im * c - re * s
            spec[k * TILE : (k + 1) * TILE, 0:LANES] = tr
            spec[k * TILE : (k + 1) * TILE, LANES : 2 * LANES] = ti
        freq = jnp.dot(
            spec[...],
            ahead[...],
            precision=lax.Precision.HIGHEST,
            preferred_element_type=jnp.float32,
        )
        number = lax.broadcasted_iota(jnp.int32, (half, TILE, 2 * LANES), 0) + first * (
            lax.broadcasted_iota(jnp.int32, (half, TILE, 2 * LANES), 2) % LANES
        )
        folded = jnp.minimum(number, circle - number)
        kept = jnp.tile(keep[slot], (1, 2))
        freq = freq.reshape(half, TILE, 2 * LANES)
        freq = jnp.where(folded < kept[None], freq, 0.0).reshape(half * TILE, 2 * LANES)
        spec[...] = jnp.dot(
            freq,
            behind[...],
            precision=lax.Precision.HIGHEST,
            preferred_element_type=jnp.float32,
        )
        turned = []
        for k in range(half):
            re = spec[k * TILE : (k + 1) * TILE, 0:LANES]
            im = spec[k * TILE : (k + 1) * TILE, LANES : 2 * LANES]
            c, s = twist[0, k : k + 1, :], twist[1, k : k + 1, :]
            turned.append((re * c - im * s, re * s + im * c))
        signal = inverse_real(turned)
        for a in range(first):
            made[slot, :, a * LANES : (a + 1) * LANES] = signal[a]
        for w in range(plan.workers):
            for index, (b, c, f) in enumerate(plan.slots[w]):

                @pl.when((band == w) & (slot == index))
                def _():
                    for hop in list(range(1, lon_count)) + [0]:
                        peer = lax.rem(lon + hop, lon_count)
                        cols = pl.ds(pl.multiple_of(peer * col_count, LANES), col_count)
                        start = pl.multiple_of(chunk_row(b, c) + lon * TILE, TILE)
                        source = made.at[index, :, cols]
                        target = back.at[f, pl.ds(start, TILE), :]
                        if hop == 0 and w == b:
                            pltpu.make_async_copy(source, target, home.at[f]).start()
                        else:
                            pltpu.make_async_remote_copy(
                                src_ref=source,
                                dst_ref=target,
                                send_sem=returned.at[index],
                                recv_sem=home.at[f],
                                device_id=(real_band(b), peer),
                                device_id_type=MESH,
                            ).start()

        return 0

    lax.fori_loop(0, slot_count, one, 0)

    for b in range(len(plan.chunks)):

        @pl.when(band == b)
        def _():
            for c in range(plan.chunks[b]):
                for f in range(6):
                    worker, _ = plan.where[b, c, f]
                    count = lon_count - 1 if worker == b else lon_count
                    span = tend.at[f, 0 : count * TILE, :]
                    pltpu.make_async_copy(span, span, sent.at[c * 6 + f]).wait()
            for f in range(6):
                span = back.at[f, 0 : plan.chunks[b] * plan.chunk, :]
                pltpu.make_async_copy(span, span, home.at[f]).wait()

    for w in range(plan.workers):
        if not plan.slots[w]:
            continue

        @pl.when(band == w)
        def _():
            for index, (b, _, _) in enumerate(plan.slots[w]):
                count = lon_count - 1 if w == b else lon_count
                span = made.at[index, :, 0 : count * col_count]
                pltpu.make_async_copy(span, span, returned.at[index]).wait()


def cap_filter(plan, tend, keep, ahead, behind, twist):
    row_count, col_count = tend.shape[1:]
    circle = col_count * lax.axis_size("lon")
    half = circle // LANES // 2 + 1
    vmem = pl.BlockSpec(memory_space=pltpu.VMEM)
    anywhere = pl.BlockSpec(memory_space=pl.ANY)
    return pl.pallas_call(
        functools.partial(filter_kernel, plan),
        out_shape=jax.ShapeDtypeStruct(tend.shape, jnp.float32),
        in_specs=[anywhere, vmem, vmem, vmem, vmem],
        out_specs=anywhere,
        scratch_shapes=[
            pltpu.VMEM((plan.most, TILE, circle), jnp.float32),
            pltpu.VMEM((plan.most, TILE, circle), jnp.float32),
            pltpu.VMEM((half * TILE, 2 * LANES), jnp.float32),
            pltpu.SemaphoreType.DMA((6 * max(plan.chunks),)),
            pltpu.SemaphoreType.DMA((plan.most,)),
            pltpu.SemaphoreType.DMA((plan.most,)),
            pltpu.SemaphoreType.DMA((6,)),
        ],
        compiler_params=pltpu.CompilerParams(
            collective_id=0, has_side_effects=True, vmem_limit_bytes=LIMIT
        ),
        name="cap_filter",
    )(tend, keep, ahead, behind, twist)


def kept_counts(plan, cutoffs, row_count, total_rows, polar):
    lat_count = lax.axis_size("lat")
    starts = np.zeros((lat_count, plan.most), np.int32)
    for lat in range(lat_count):
        north = lat >= lat_count // 2
        band = lat_count - 1 - lat if north else lat
        for slot, (b, c, _) in enumerate(plan.slots[band]):
            base = row_count - plan.chunks[b] * plan.chunk if north else 0
            real = lat_count - 1 - b if north else b
            starts[lat, slot] = real * row_count + base + c * plan.chunk
    start = lax.dynamic_index_in_dim(jnp.asarray(starts), lax.axis_index("lat"), keepdims=False)
    rows = (
        start[:, None]
        + lax.axis_index("lon") * TILE
        + jnp.arange(TILE, dtype=jnp.int32)[None, :]
    ).reshape(-1)
    position = jnp.where(rows < polar, rows, rows - (total_rows - 2 * polar))
    ids = jnp.arange(2 * polar, dtype=jnp.int32)
    counts = jnp.sum(
        jnp.where(position[:, None] == ids[None, :], cutoffs[None, :], 0), axis=1, dtype=jnp.int32
    )
    return jnp.broadcast_to(counts.reshape(plan.most, TILE, 1), (plan.most, TILE, LANES))


def geometry(row_start, row_count, total_rows):
    ids = row_start - TILE + jnp.arange(row_count + 2 * TILE, dtype=jnp.int32)
    spacing = math.pi / total_rows
    centre = -0.5 * math.pi + (ids.astype(jnp.float32) + 0.5) * spacing
    face = -0.5 * math.pi + (ids.astype(jnp.float32) + 1.0) * spacing
    live = jnp.where((ids >= 0) & (ids < total_rows - 1), 1.0, 0.0).astype(jnp.float32)
    centre_cos = jnp.cos(centre)
    face_cos = jnp.cos(face) * live
    face_inverse = live / (face_cos + (1.0 - live))
    coefs = jnp.stack(
        [centre_cos, 1.0 / centre_cos, face_cos, CORIOLIS * jnp.sin(face), face_inverse, live]
    )
    return jnp.broadcast_to(coefs[:, :, None], coefs.shape + (LANES,))


def rims(fields):
    lat_count, lon_count = lax.axis_size("lat"), lax.axis_size("lon")
    up = [(i, i + 1) for i in range(lat_count - 1)]
    down = [(i + 1, i) for i in range(lat_count - 1)]
    south = lax.ppermute(fields[:, -1:, :], "lat", up)
    north = lax.ppermute(fields[:, :1, :], "lat", down)
    right = [(i, (i + 1) % lon_count) for i in range(lon_count)]
    left = [((i + 1) % lon_count, i) for i in range(lon_count)]
    last = jnp.concatenate([south[:, :, -1:], fields[:, :, -1:], north[:, :, -1:]], axis=1)
    head = jnp.concatenate([south[:, :, :1], fields[:, :, :1], north[:, :, :1]], axis=1)
    west = lax.ppermute(last[:, :, 0], "lon", right)
    east = lax.ppermute(head[:, :, 0], "lon", left)
    rows = jnp.concatenate(
        [
            jnp.pad(south, ((0, 0), (TILE - 1, 0), (0, 0))),
            jnp.pad(north, ((0, 0), (0, TILE - 1), (0, 0))),
        ],
        axis=1,
    )
    edge = ((0, 0), (TILE - 1, TILE - 1))
    west, east = jnp.pad(west, edge), jnp.pad(east, edge)
    lane = jnp.arange(2 * LANES, dtype=jnp.int32)
    cols = jnp.where(lane == LANES - 1, west[:, :, None], jnp.where(lane == LANES, east[:, :, None], 0.0))
    return rows, cols


def body(thickness, winds, terrain, cutoffs):
    row_count = thickness.shape[1]
    col_count = thickness.shape[2]
    lat_count, lon_count = lax.axis_size("lat"), lax.axis_size("lon")
    total_rows = row_count * lat_count
    circle = col_count * lon_count
    polar = (total_rows + 2) // 6
    plan = Plan(lat_count, lon_count, row_count, polar)
    row_start = lax.axis_index("lat") * row_count
    global_rows = row_start + jnp.arange(row_count, dtype=jnp.int32)
    live = jnp.where(global_rows < total_rows - 1, 1.0, 0.0).astype(jnp.float32)
    capped = ((global_rows < polar) | (global_rows >= total_rows - polar))[None, :, None]
    coefs = geometry(row_start, row_count, total_rows)
    keep = kept_counts(plan, cutoffs, row_count, total_rows, polar)
    ahead, behind, twist = [jnp.asarray(x) for x in tables(circle)]
    current = jnp.concatenate([thickness, winds[0], winds[1] * live[None, :, None]], axis=0)
    step_size = 0.1 * min(1.0, circle / (2.0 * total_rows))
    anchor = current
    ground_rows, ground_cols = rims(terrain[None])
    for fraction in (1.0 / 3.0, 0.5, 1.0):
        rows, cols = rims(current)
        rows = jnp.concatenate([rows, ground_rows], axis=0)
        cols = jnp.concatenate([cols, ground_cols], axis=0)
        tendency = stencil(current, rows, cols, terrain, coefs)
        filtered = cap_filter(plan, tendency, keep, ahead, behind, twist)
        current = anchor + fraction * step_size * jnp.where(capped, filtered, tendency)
    return (current[0:2], current[2:6].reshape(2, 2, row_count, col_count))


def solution(mesh):
    in_specs = (P(None, "lat", "lon"), P(None, None, "lat", "lon"), P("lat", "lon"), P())
    out_specs = (P(None, "lat", "lon"), P(None, None, "lat", "lon"))
    return jax.shard_map(body, mesh=mesh, in_specs=in_specs, out_specs=out_specs, check_vma=False)
```
